512 devices in a mesh: res: 64 (over z_hi, x, y), seq: 8 (over z_lo, core).
Axes of the slice: x: 4, y: 8, z: 8 (z_hi: 2, z_lo: 4; z = z_hi * 4 + z_lo), core: 2. Of those that a mesh axis runs over, the one named last changes fastest.
Arguments:
- alignment_features: float32 [512, 512, 256], P('seq', 'res'), may hold values from -8 to 8
- layer_norm_gain: float32 [256], replicated, may hold values from 0.5 to 2
- left_projection_weight: float32 [256, 32], replicated, may hold values from -0.375 to 0.375
- right_projection_weight: float32 [256, 32], replicated, may hold values from -0.375 to 0.375
- output_projection_weight: float32 [1024, 128], replicated, may hold values from -0.1875 to 0.1875
- output_bias_vector: float32 [128], replicated, may hold values from -3 to 3
Outputs:
- pair_tiles: float32 [4, 512, 8, 128], P(None, 'res', 'seq')
The draws below stay inside these ranges and needn't reach their ends.
All inputs are finite; a program needn't handle non-finite values.
Results may differ from the reference program's by a relative error of at most 0.0003.
Values sent between devices are 32-bit elements; how exact they have to be, the bound alone decides.
A program may use at most 64 MiB of HBM per device.

```python
import math
import jax
import jax.numpy as jnp
from jax import lax

C = 256
PW = 32
CZ = 128
R_DEV = 8
ROUNDS = 4
R = 512
S = 512
N_RES = 64


def draw_alignment_features(key, part):
    key_profile, key_noise = jax.random.split(key)
    profile = jnp.clip(jax.random.normal(key_profile, (R, C), jnp.float32), -4.0, 4.0)
    seq_noise = jnp.clip(jax.random.normal(key_noise, (S, R, C), jnp.float32), -4.0, 4.0)
    return (profile[None, :, :] + seq_noise).astype(jnp.float32)


def normal_values(key, dims, spread, limit, held_as=jnp.bfloat16):
    result = spread * jax.random.normal(key, dims, jnp.float32)
    return jnp.clip(result, min=-limit, max=limit).astype(held_as)


def setup_inputs(seed: int = 0) -> dict:
    key_of = jax.random.split(jax.random.key(seed), 7)
    alignment_features = draw_alignment_features(jax.random.fold_in(key_of[6], 71), 0)
    layer_norm_gain = jnp.clip(jnp.exp(jax.random.uniform(key_of[1], (C,), jnp.float32, math.log(0.5), math.log(2.0))), 0.5, 2.0)
    left_projection_weight = normal_values(key_of[2], (C, PW), C ** -0.5, 0.375, jnp.float32)
    right_projection_weight = normal_values(key_of[3], (C, PW), C ** -0.5, 0.375, jnp.float32)
    output_projection_weight = normal_values(key_of[4], (PW * PW, CZ), (PW * PW) ** -0.5, 0.1875, jnp.float32)
    output_bias_vector = normal_values(key_of[5], (CZ,), 0.5, 3.0, jnp.float32)
    return {"alignment_features": alignment_features, "layer_norm_gain": layer_norm_gain, "left_projection_weight": left_projection_weight, "right_projection_weight": right_projection_weight, "output_projection_weight": output_projection_weight, "output_bias_vector": output_bias_vector}


def apply_layer_norm(features, layer_norm_gain):
    row_mean = lax.optimization_barrier(jnp.mean(features, axis=-1, keepdims=True))
    centered = features - row_mean
    variance = lax.optimization_barrier(jnp.mean(centered * centered, axis=-1, keepdims=True))
    return centered * lax.rsqrt(variance + 1e-05) * layer_norm_gain

def reference(alignment_features, layer_norm_gain, left_projection_weight, right_projection_weight, output_projection_weight, output_bias_vector):
    normalized_features = apply_layer_norm(alignment_features, layer_norm_gain)
    flat_rows = normalized_features.reshape(S * R, C)
    left_proj = jnp.dot(flat_rows, left_projection_weight, precision=lax.Precision.HIGHEST).reshape(S, N_RES, R_DEV, PW)
    right_proj = jnp.dot(flat_rows, right_projection_weight, precision=lax.Precision.HIGHEST).reshape(S, N_RES, R_DEV, PW)
    block_ids = jnp.arange(N_RES, dtype=jnp.int32)
    tiles_all = []
    for step in range(ROUNDS):

        def one_block(block):
            partner = jnp.bitwise_xor(block, jnp.int32(1 << step)).astype(jnp.int32)
            left_part = lax.dynamic_index_in_dim(left_proj, block, 1, keepdims=False)
            right_part = lax.dynamic_index_in_dim(right_proj, partner, 1, keepdims=False)
            outer_sum = jnp.einsum('sxc,syd->xycd', left_part, right_part, precision=lax.Precision.HIGHEST) / S
            projected = jnp.dot(outer_sum.reshape(R_DEV * R_DEV, PW * PW), output_projection_weight, precision=lax.Precision.HIGHEST)
            return projected.reshape(R_DEV, R_DEV, CZ) + output_bias_vector
        tiles = lax.map(one_block, block_ids)
        tiles_all.append(tiles.reshape(R, R_DEV, CZ))
    return jnp.stack(tiles_all)
```

```python
import jax
import jax.numpy as jnp
from jax import lax
from jax.experimental import pallas as pl
from jax.experimental.pallas import tpu as pltpu
from jax.sharding import PartitionSpec as P

ROUNDS = 4
CHUNKS = 4
ROUND_ORDER = (3, 0, 1, 2)


def split(value):
    high = value.astype(jnp.bfloat16)
    low = (value - high.astype(jnp.float32)).astype(jnp.bfloat16)
    return high, low


def matmul(a, b):
    return lax.dot_general(a, b, (((1,), (0,)), ((), ())), preferred_element_type=jnp.float32)


def matmul_nt(a, b):
    return lax.dot_general(a, b, (((1,), (1,)), ((), ())), preferred_element_type=jnp.float32)


def group_index(rows, width):
    return lax.broadcasted_iota(jnp.int32, (rows, 128), 1) // width


def pick(parts, group):
    result = parts[-1]
    for index in range(len(parts) - 2, -1, -1):
        result = jnp.where(group == index, parts[index], result)
    return result


def kernel(
    features_hbm,
    gain_hbm,
    left_hbm,
    right_hbm,
    weight_hbm,
    bias_hbm,
    out_ref,
    features,
    gain,
    left_weight,
    right_weight,
    weight,
    bias,
    in_sem,
    proj_high,
    proj_low,
    weight_split,
    left_rows,
    right_rows,
    left_turned,
    left_parts,
    right_mine,
    right_got,
    outer,
    tiles,
    sums,
    right_send_sem,
    right_recv_sem,
    sum_send_sem,
    sum_recv_sem,
):
    rows = features.shape[0]
    chunk_rows = rows // CHUNKS
    chunk_seqs = chunk_rows // 8
    local_seqs = rows // 8
    hidden = 32
    seq_devices = 8
    total_seqs = local_seqs * seq_devices

    block = lax.axis_index("res")
    seq = lax.axis_index("seq")

    def partner(step):
        mask = 1 << step
        return block + mask - 2 * mask * ((block // mask) % 2)

    def peer(offset):
        return (seq + offset) % seq_devices

    loads = []
    for index, (source, target) in enumerate(
        ((left_hbm, left_weight), (right_hbm, right_weight), (gain_hbm, gain))
    ):
        loads.append(pltpu.make_async_copy(source, target, in_sem.at[index]))
    chunk_loads = []
    for chunk in range(CHUNKS):
        part = pl.ds(chunk * chunk_rows, chunk_rows)
        chunk_loads.append(
            pltpu.make_async_copy(features_hbm.at[part], features.at[part], in_sem.at[5 + chunk])
        )
    weight_load = pltpu.make_async_copy(weight_hbm, weight, in_sem.at[3])
    bias_load = pltpu.make_async_copy(bias_hbm, bias, in_sem.at[4])
    for copy in loads + chunk_loads + [weight_load, bias_load]:
        copy.start()

    barrier = pltpu.get_barrier_semaphore()
    for step in range(ROUNDS):
        pl.semaphore_signal(barrier, inc=1, device_id=(partner(step), seq))
    for offset in range(1, seq_devices):
        pl.semaphore_signal(barrier, inc=1, device_id=(block, peer(offset)))

    for copy in loads:
        copy.wait()
    left_high, left_low = split(left_weight[...] * gain[...])
    right_high, right_low = split(right_weight[...] * gain[...])
    proj_high[...] = jnp.concatenate([left_high] * 4 + [right_high] * 4, axis=0)
    proj_low[...] = jnp.concatenate([left_low] * 4 + [right_low] * 4, axis=0)

    def right_copy(step, chunk):
        part = pl.ds(chunk * chunk_seqs, chunk_seqs)
        return pltpu.make_async_remote_copy(
            src_ref=right_mine.at[part],
            dst_ref=right_got.at[step, part],
            send_sem=right_send_sem.at[step, chunk],
            recv_sem=right_recv_sem.at[step, chunk],
            device_id=(partner(step), seq),
        )

    chunk_group = group_index(chunk_seqs, hidden)
    for chunk in range(CHUNKS):
        chunk_loads[chunk].wait()
        part = pl.ds(chunk * chunk_rows, chunk_rows)
        values = features[part]
        centered = values - jnp.mean(values, axis=1, keepdims=True)
        variance = jnp.mean(centered * centered, axis=1, keepdims=True)
        high, low = split(centered * lax.rsqrt(variance + 1e-05))
        projected = (
            matmul_nt(high, proj_low[...]) + matmul_nt(low, proj_high[...])
        ) + matmul_nt(high, proj_high[...])
        left_rows[part] = projected[:, :128]
        right_rows[part] = projected[:, 128:]
        for half in range(2):
            lanes = [
                right_rows[pl.ds(chunk * chunk_rows + half * 4 + x, chunk_seqs, stride=8), :]
                for x in range(4)
            ]
            right_mine[pl.ds(chunk * chunk_seqs, chunk_seqs), pl.ds(half * 128, 128)] = pick(
                lanes, chunk_group
            )
        if chunk == 0:
            pl.semaphore_wait(barrier, ROUNDS + seq_devices - 1)
        for step in (2, 1, 0, 3):
            right_copy(step, chunk).start()

    seq_group = group_index(local_seqs, hidden)
    for half in range(2):
        lanes = [left_rows[pl.ds(half * 4 + x, local_seqs, stride=8), :] for x in range(4)]
        left_half = pick(lanes, seq_group) * (1.0 / total_seqs)
        left_turned[pl.ds(half * 128, 128), :] = jnp.concatenate([left_half, left_half], axis=0).T
    left_columns = jnp.concatenate(
        [left_turned[pl.ds(c, 8, stride=hidden), :] for c in range(hidden)], axis=0
    )
    turned_high, turned_low = split(left_columns)
    left_parts[...] = jnp.concatenate([turned_high, turned_low], axis=1)

    weight_load.wait()
    bias_load.wait()
    weight_high, weight_low = split(weight[...])
    weight_split[...] = jnp.concatenate([weight_high, weight_low], axis=1)

    def sum_copy(step, offset):
        return pltpu.make_async_remote_copy(
            src_ref=tiles.at[step, peer(offset)],
            dst_ref=sums.at[step, offset - 1],
            send_sem=sum_send_sem.at[step, offset - 1],
            recv_sem=sum_recv_sem.at[step, offset - 1],
            device_id=(block, peer(offset)),
        )

    group = group_index(8, hidden)
    for step in ROUND_ORDER:
        for chunk in range(CHUNKS):
            right_copy(step, chunk).wait_recv()
        right_high, right_low = split(right_got[step])
        outer[...] = matmul(
            left_parts[...],
            jnp.concatenate([right_high, right_low, right_high, right_low], axis=0),
        )
        pieces = []
        for y_half in range(2):
            columns = [[None] * 8 for _ in range(4)]
            for c_quad in range(8):
                turned = [
                    outer[pl.ds((c_quad * 4 + i) * 8, 8), pl.ds(y_half * 128, 128)]
                    for i in range(4)
                ]
                turned = [turned[0]] + [pltpu.roll(turned[i], 32 * i, 1) for i in range(1, 4)]
                for y in range(4):
                    mixed = pick([turned[(g - y) % 4] for g in range(4)], group)
                    if y:
                        mixed = pltpu.roll(mixed, 128 - 32 * y, 1)
                    columns[y][c_quad] = mixed
            for y in range(4):
                pieces.append(jnp.concatenate(columns[y], axis=1))
        flat_high, flat_low = split(jnp.concatenate(pieces, axis=0))
        product = matmul(jnp.concatenate([flat_high, flat_low], axis=0), weight_split[...])
        total = (product[64:, 128:] + product[64:, :128]) + (product[:64, 128:] + product[:64, :128])
        tiles[step] = total.reshape(8, 8, 128)
        for offset in range(1, seq_devices):
            sum_copy(step, offset).start()

    for step in ROUND_ORDER:
        for offset in range(1, seq_devices):
            sum_copy(step, offset).wait_recv()
        total = tiles[step, seq] + bias[...]
        for offset in range(1, seq_devices):
            total = total + sums[step, offset - 1]
        out_ref[step] = total

    for step in range(ROUNDS):
        for chunk in range(CHUNKS):
            right_copy(step, chunk).wait_send()
        for offset in range(1, seq_devices):
            sum_copy(step, offset).wait_send()


def on_device(features, gain, left_weight, right_weight, weight, bias):
    local_seqs, residues, channels = features.shape
    rows = local_seqs * residues
    f32, bf16 = jnp.float32, jnp.bfloat16
    dma = pltpu.SemaphoreType.DMA
    out = pl.pallas_call(
        kernel,
        out_shape=jax.ShapeDtypeStruct((ROUNDS, 8, 128), f32),
        in_specs=[pl.BlockSpec(memory_space=pltpu.HBM)] * 6,
        out_specs=pl.BlockSpec(memory_space=pltpu.VMEM),
        scratch_shapes=[
            pltpu.VMEM((rows, channels), f32),
            pltpu.VMEM((1, channels), f32),
            pltpu.VMEM((32, channels), f32),
            pltpu.VMEM((32, channels), f32),
            pltpu.VMEM((1024, 128), f32),
            pltpu.VMEM((1, 128), f32),
            dma((5 + CHUNKS,)),
            pltpu.VMEM((256, channels), bf16),
            pltpu.VMEM((256, channels), bf16),
            pltpu.VMEM((1024, 256), bf16),
            pltpu.VMEM((rows, 128), f32),
            pltpu.VMEM((rows, 128), f32),
            pltpu.VMEM((256, 128), f32),
            pltpu.VMEM((256, 256), bf16),
            pltpu.VMEM((local_seqs, 256), f32),
            pltpu.VMEM((ROUNDS, local_seqs, 256), f32),
            pltpu.VMEM((256, 256), f32),
            pltpu.VMEM((ROUNDS, 8, 8, 128), f32),
            pltpu.VMEM((ROUNDS, 7, 8, 128), f32),
            dma((ROUNDS, CHUNKS)),
            dma((ROUNDS, CHUNKS)),
            dma((ROUNDS, 7)),
            dma((ROUNDS, 7)),
        ],
        compiler_params=pltpu.CompilerParams(
            collective_id=0, has_side_effects=True, vmem_limit_bytes=32 * 1024 * 1024
        ),
    )(
        features.reshape(rows, channels),
        gain.reshape(1, channels),
        left_weight.T,
        right_weight.T,
        weight,
        bias.reshape(1, 128),
    )
    return out.reshape(ROUNDS, 8, 1, 128)


def solution(mesh):
    in_specs = (P("seq", "res", None), P(), P(), P(), P(), P())
    out_specs = P(None, "res", "seq", None)
    return jax.shard_map(
        on_device, mesh=mesh, in_specs=in_specs, out_specs=out_specs, check_vma=False
    )
```

```python
import jax
import jax.numpy as jnp
from jax import lax
from jax.experimental import pallas as pl
from jax.experimental.pallas import tpu as pltpu
from jax.sharding import PartitionSpec as P

ROUNDS = 4
CHUNKS = 2
ROUND_ORDER = (3, 2, 1, 0)
PEERS = (6, 7, 4, 5, 2, 3, 1)


def split(value):
    high = value.astype(jnp.bfloat16)
    low = (value - high.astype(jnp.float32)).astype(jnp.bfloat16)
    return high, low


def matmul(a, b):
    return lax.dot_general(a, b, (((1,), (0,)), ((), ())), preferred_element_type=jnp.float32)


def matmul_nt(a, b):
    return lax.dot_general(a, b, (((1,), (1,)), ((), ())), preferred_element_type=jnp.float32)


def group_index(rows, width):
    return lax.broadcasted_iota(jnp.int32, (rows, 128), 1) // width


def pick(parts, group):
    result = parts[-1]
    for index in range(len(parts) - 2, -1, -1):
        result = jnp.where(group == index, parts[index], result)
    return result


def kernel(
    features_hbm,
    gain_hbm,
    left_hbm,
    right_hbm,
    weight_hbm,
    bias_hbm,
    out_ref,
    features,
    gain,
    left_weight,
    right_weight,
    weight,
    bias,
    in_sem,
    proj_high,
    proj_low,
    weight_split,
    left_rows,
    right_rows,
    left_turned,
    left_parts,
    right_mine,
    right_got,
    outer,
    tiles,
    sums,
    right_send_sem,
    right_recv_sem,
    sum_send_sem,
    sum_recv_sem,
):
    rows = features.shape[0]
    chunk_rows = rows // CHUNKS
    chunk_seqs = chunk_rows // 8
    local_seqs = rows // 8
    hidden = 32
    seq_devices = 8
    total_seqs = local_seqs * seq_devices

    block = lax.axis_index("res")
    seq = lax.axis_index("seq")

    def flip(index, mask):
        return index + mask - 2 * mask * ((index // mask) % 2)

    def partner(step):
        return flip(block, 1 << step)

    def peer(offset):
        result = seq
        for mask in (1, 2, 4):
            if offset & mask:
                result = flip(result, mask)
        return result

    loads = []
    for index, (source, target) in enumerate(
        ((left_hbm, left_weight), (right_hbm, right_weight), (gain_hbm, gain))
    ):
        loads.append(pltpu.make_async_copy(source, target, in_sem.at[index]))
    chunk_loads = []
    for chunk in range(CHUNKS):
        part = pl.ds(chunk * chunk_rows, chunk_rows)
        chunk_loads.append(
            pltpu.make_async_copy(features_hbm.at[part], features.at[part], in_sem.at[5 + chunk])
        )
    weight_load = pltpu.make_async_copy(weight_hbm, weight, in_sem.at[3])
    bias_load = pltpu.make_async_copy(bias_hbm, bias, in_sem.at[4])
    for copy in loads + chunk_loads + [weight_load, bias_load]:
        copy.start()

    barrier = pltpu.get_barrier_semaphore()
    for step in range(ROUNDS):
        pl.semaphore_signal(barrier, inc=1, device_id=(partner(step), seq))
    for offset in range(1, seq_devices):
        pl.semaphore_signal(barrier, inc=1, device_id=(block, peer(offset)))

    for copy in loads:
        copy.wait()
    left_high, left_low = split(left_weight[...] * gain[...])
    right_high, right_low = split(right_weight[...] * gain[...])
    proj_high[...] = jnp.concatenate([left_high] * 4 + [right_high] * 4, axis=0)
    proj_low[...] = jnp.concatenate([left_low] * 4 + [right_low] * 4, axis=0)

    def right_copy(step, chunk):
        part = pl.ds(chunk * chunk_seqs, chunk_seqs)
        return pltpu.make_async_remote_copy(
            src_ref=right_mine.at[part],
            dst_ref=right_got.at[step, part],
            send_sem=right_send_sem.at[step, chunk],
            recv_sem=right_recv_sem.at[step, chunk],
            device_id=(partner(step), seq),
        )

    chunk_group = group_index(chunk_seqs, hidden)
    for chunk in range(CHUNKS):
        chunk_loads[chunk].wait()
        part = pl.ds(chunk * chunk_rows, chunk_rows)
        values = features[part]
        centered = values - jnp.mean(values, axis=1, keepdims=True)
        variance = jnp.mean(centered * centered, axis=1, keepdims=True)
        high, low = split(centered * lax.rsqrt(variance + 1e-05))
        projected = (
            matmul_nt(high, proj_low[...]) + matmul_nt(low, proj_high[...])
        ) + matmul_nt(high, proj_high[...])
        left_rows[part] = projected[:, :128]
        right_rows[part] = projected[:, 128:]
        for half in range(2):
            lanes = [
                right_rows[pl.ds(chunk * chunk_rows + half * 4 + x, chunk_seqs, stride=8), :]
                for x in range(4)
            ]
            right_mine[pl.ds(chunk * chunk_seqs, chunk_seqs), pl.ds(half * 128, 128)] = pick(
                lanes, chunk_group
            )
        if chunk == 0:
            pl.semaphore_wait(barrier, ROUNDS + seq_devices - 1)
        for step in (2, 3):
            right_copy(step, chunk).start()
    for step in (1, 0):
        for chunk in range(CHUNKS):
            right_copy(step, chunk).start()

    seq_group = group_index(local_seqs, hidden)
    for half in range(2):
        lanes = [left_rows[pl.ds(half * 4 + x, local_seqs, stride=8), :] for x in range(4)]
        left_half = pick(lanes, seq_group) * (1.0 / total_seqs)
        left_turned[pl.ds(half * 128, 128), :] = jnp.concatenate([left_half, left_half], axis=0).T
    left_columns = jnp.concatenate(
        [left_turned[pl.ds(c, 8, stride=hidden), :] for c in range(hidden)], axis=0
    )
    turned_high, turned_low = split(left_columns)
    left_parts[...] = jnp.concatenate([turned_high, turned_low], axis=1)

    weight_load.wait()
    bias_load.wait()
    weight_high, weight_low = split(weight[...])
    weight_split[...] = jnp.concatenate([weight_high, weight_low], axis=1)

    def sum_copy(step, offset):
        return pltpu.make_async_remote_copy(
            src_ref=tiles.at[step, peer(offset)],
            dst_ref=sums.at[step, offset - 1],
            send_sem=sum_send_sem.at[step, offset - 1],
            recv_sem=sum_recv_sem.at[step, offset - 1],
            device_id=(block, peer(offset)),
        )

    group = group_index(8, hidden)
    for step in ROUND_ORDER:
        for chunk in range(CHUNKS):
            right_copy(step, chunk).wait_recv()
        right_high, right_low = split(right_got[step])
        outer[...] = matmul(
            left_parts[...],
            jnp.concatenate([right_high, right_low, right_high, right_low], axis=0),
        )
        pieces = []
        for y_half in range(2):
            columns = [[None] * 8 for _ in range(4)]
            for c_quad in range(8):
                turned = [
                    outer[pl.ds((c_quad * 4 + i) * 8, 8), pl.ds(y_half * 128, 128)]
                    for i in range(4)
                ]
                turned = [turned[0]] + [pltpu.roll(turned[i], 32 * i, 1) for i in range(1, 4)]
                for y in range(4):
                    mixed = pick([turned[(g - y) % 4] for g in range(4)], group)
                    if y:
                        mixed = pltpu.roll(mixed, 128 - 32 * y, 1)
                    columns[y][c_quad] = mixed
            for y in range(4):
                pieces.append(jnp.concatenate(columns[y], axis=1))
        flat_high, flat_low = split(jnp.concatenate(pieces, axis=0))
        product = matmul(jnp.concatenate([flat_high, flat_low], axis=0), weight_split[...])
        total = (product[64:, 128:] + product[64:, :128]) + (product[:64, 128:] + product[:64, :128])
        tiles[step] = total.reshape(8, 8, 128)
        for offset in PEERS:
            sum_copy(step, offset).start()

    for step in ROUND_ORDER:
        for offset in range(1, seq_devices):
            sum_copy(step, offset).wait_recv()
        total = tiles[step, seq] + bias[...]
        for offset in range(1, seq_devices):
            total = total + sums[step, offset - 1]
        out_ref[step] = total

    for step in range(ROUNDS):
        for chunk in range(CHUNKS):
            right_copy(step, chunk).wait_send()
        for offset in range(1, seq_devices):
            sum_copy(step, offset).wait_send()


def on_device(features, gain, left_weight, right_weight, weight, bias):
    local_seqs, residues, channels = features.shape
    rows = local_seqs * residues
    f32, bf16 = jnp.float32, jnp.bfloat16
    dma = pltpu.SemaphoreType.DMA
    out = pl.pallas_call(
        kernel,
        out_shape=pltpu.VMEM((ROUNDS, 8, 128), f32),
        in_specs=[pl.BlockSpec(memory_space=pltpu.HBM)] * 6,
        out_specs=pl.BlockSpec(memory_space=pltpu.VMEM),
        scratch_shapes=[
            pltpu.VMEM((rows, channels), f32),
            pltpu.VMEM((1, channels), f32),
            pltpu.VMEM((32, channels), f32),
            pltpu.VMEM((32, channels), f32),
            pltpu.VMEM((1024, 128), f32),
            pltpu.VMEM((1, 128), f32),
            dma((5 + CHUNKS,)),
            pltpu.VMEM((256, channels), bf16),
            pltpu.VMEM((256, channels), bf16),
            pltpu.VMEM((1024, 256), bf16),
            pltpu.VMEM((rows, 128), f32),
            pltpu.VMEM((rows, 128), f32),
            pltpu.VMEM((256, 128), f32),
            pltpu.VMEM((256, 256), bf16),
            pltpu.VMEM((local_seqs, 256), f32),
            pltpu.VMEM((ROUNDS, local_seqs, 256), f32),
            pltpu.VMEM((256, 256), f32),
            pltpu.VMEM((ROUNDS, 8, 8, 128), f32),
            pltpu.VMEM((ROUNDS, 7, 8, 128), f32),
            dma((ROUNDS, CHUNKS)),
            dma((ROUNDS, CHUNKS)),
            dma((ROUNDS, 7)),
            dma((ROUNDS, 7)),
        ],
        compiler_params=pltpu.CompilerParams(
            collective_id=0, has_side_effects=True, vmem_limit_bytes=32 * 1024 * 1024
        ),
    )(
        *(
            pltpu.with_memory_space_constraint(operand, pltpu.HBM)
            for operand in (
                features.reshape(rows, channels),
                gain.reshape(1, channels),
                left_weight.T,
                right_weight.T,
                weight,
                bias.reshape(1, 128),
            )
        )
    )
    return out.reshape(ROUNDS, 8, 1, 128)


def solution(mesh):
    in_specs = (P("seq", "res", None), P(), P(), P(), P(), P())
    out_specs = P(None, "res", "seq", None)
    return jax.shard_map(
        on_device, mesh=mesh, in_specs=in_specs, out_specs=out_specs, check_vma=False
    )
```

```python
import jax
import jax.numpy as jnp
from jax import lax
from jax.experimental import pallas as pl
from jax.experimental.pallas import tpu as pltpu
from jax.sharding import PartitionSpec as P

ROUNDS = 4
SEND_ORDER = (3, 2, 1, 0)
ROUND_ORDER = (3, 2, 1, 0)
PEERS = (6, 7, 4, 5, 2, 3, 1)


def split(value):
    high = value.astype(jnp.bfloat16)
    low = (value - high.astype(jnp.float32)).astype(jnp.bfloat16)
    return high, low


def matmul(a, b):
    return lax.dot_general(a, b, (((1,), (0,)), ((), ())), preferred_element_type=jnp.float32)


def matmul_nt(a, b):
    return lax.dot_general(a, b, (((1,), (1,)), ((), ())), preferred_element_type=jnp.float32)


def group_index(rows, width):
    return lax.broadcasted_iota(jnp.int32, (rows, 128), 1) // width


def pick(parts, group):
    result = parts[-1]
    for index in range(len(parts) - 2, -1, -1):
        result = jnp.where(group == index, parts[index], result)
    return result


def kernel(
    features_hbm,
    gain_hbm,
    left_hbm,
    right_hbm,
    weight_hbm,
    bias_hbm,
    out_ref,
    features,
    gain,
    left_weight,
    right_weight,
    weight,
    bias,
    in_sem,
    proj_high,
    proj_low,
    weight_split,
    left_rows,
    right_rows,
    left_turned,
    left_parts,
    right_mine,
    right_got,
    outer,
    tiles,
    sums,
    right_send_sem,
    right_recv_sem,
    sum_send_sem,
    sum_recv_sem,
):
    rows = features.shape[0]
    local_seqs = rows // 8
    hidden = 32
    seq_devices = 8
    total_seqs = local_seqs * seq_devices

    block = lax.axis_index("res")
    seq = lax.axis_index("seq")

    def flip(index, mask):
        return index + mask - 2 * mask * ((index // mask) % 2)

    def partner(step):
        return flip(block, 1 << step)

    def peer(offset):
        result = seq
        for mask in (1, 2, 4):
            if offset & mask:
                result = flip(result, mask)
        return result

    copies = [
        pltpu.make_async_copy(source, target, in_sem.at[index])
        for index, (source, target) in enumerate(
            (
                (features_hbm, features),
                (left_hbm, left_weight),
                (right_hbm, right_weight),
                (gain_hbm, gain),
                (weight_hbm, weight),
                (bias_hbm, bias),
            )
        )
    ]
    for copy in copies:
        copy.start()

    barrier = pltpu.get_barrier_semaphore()
    for step in range(ROUNDS):
        pl.semaphore_signal(barrier, inc=1, device_id=(partner(step), seq))
    for offset in range(1, seq_devices):
        pl.semaphore_signal(barrier, inc=1, device_id=(block, peer(offset)))

    for copy in copies[1:4]:
        copy.wait()
    left_high, left_low = split(left_weight[...] * gain[...])
    right_high, right_low = split(right_weight[...] * gain[...])
    proj_high[...] = jnp.concatenate([left_high] * 4 + [right_high] * 4, axis=0)
    proj_low[...] = jnp.concatenate([left_low] * 4 + [right_low] * 4, axis=0)

    def right_copy(step):
        return pltpu.make_async_remote_copy(
            src_ref=right_mine,
            dst_ref=right_got.at[step],
            send_sem=right_send_sem,
            recv_sem=right_recv_sem.at[step],
            device_id=(partner(step), seq),
        )

    copies[0].wait()
    values = features[...]
    centered = values - jnp.mean(values, axis=1, keepdims=True)
    variance = jnp.mean(centered * centered, axis=1, keepdims=True)
    high, low = split(centered * lax.rsqrt(variance + 1e-05))
    projected = (
        matmul_nt(high, proj_low[...]) + matmul_nt(low, proj_high[...])
    ) + matmul_nt(high, proj_high[...])
    left_rows[...] = projected[:, :128]
    right_rows[...] = projected[:, 128:]
    seq_group = group_index(local_seqs, hidden)
    for half in range(2):
        lanes = [right_rows[pl.ds(half * 4 + x, local_seqs, stride=8), :] for x in range(4)]
        right_mine[:, pl.ds(half * 128, 128)] = pick(lanes, seq_group)
    pl.semaphore_wait(barrier, ROUNDS + seq_devices - 1)
    for step in SEND_ORDER:
        right_copy(step).start()

    for half in range(2):
        lanes = [left_rows[pl.ds(half * 4 + x, local_seqs, stride=8), :] for x in range(4)]
        left_half = pick(lanes, seq_group) * (1.0 / total_seqs)
        left_turned[pl.ds(half * 128, 128), :] = jnp.concatenate([left_half, left_half], axis=0).T
    left_columns = jnp.concatenate(
        [left_turned[pl.ds(c, 8, stride=hidden), :] for c in range(hidden)], axis=0
    )
    turned_high, turned_low = split(left_columns)
    left_parts[...] = jnp.concatenate([turned_high, turned_low], axis=1)

    for copy in copies[4:]:
        copy.wait()
    weight_high, weight_low = split(weight[...])
    weight_split[...] = jnp.concatenate([weight_high, weight_low], axis=1)

    def sum_copy(step, offset):
        return pltpu.make_async_remote_copy(
            src_ref=tiles.at[step, peer(offset)],
            dst_ref=sums.at[step, offset - 1],
            send_sem=sum_send_sem,
            recv_sem=sum_recv_sem,
            device_id=(block, peer(offset)),
        )

    group = group_index(8, hidden)
    for step in ROUND_ORDER:
        right_copy(step).wait_recv()
        right_high, right_low = split(right_got[step])
        outer[...] = matmul(
            left_parts[...],
            jnp.concatenate([right_high, right_low, right_high, right_low], axis=0),
        )
        pieces = []
        for y_half in range(2):
            columns = [[None] * 8 for _ in range(4)]
            for c_quad in range(8):
                turned = [
                    outer[pl.ds((c_quad * 4 + i) * 8, 8), pl.ds(y_half * 128, 128)]
                    for i in range(4)
                ]
                turned = [turned[0]] + [pltpu.roll(turned[i], 32 * i, 1) for i in range(1, 4)]
                for y in range(4):
                    mixed = pick([turned[(g - y) % 4] for g in range(4)], group)
                    if y:
                        mixed = pltpu.roll(mixed, 128 - 32 * y, 1)
                    columns[y][c_quad] = mixed
            for y in range(4):
                pieces.append(jnp.concatenate(columns[y], axis=1))
        flat_high, flat_low = split(jnp.concatenate(pieces, axis=0))
        product = matmul(jnp.concatenate([flat_high, flat_low], axis=0), weight_split[...])
        total = (product[64:, 128:] + product[64:, :128]) + (product[:64, 128:] + product[:64, :128])
        tiles[step] = total.reshape(8, 8, 128)
        for offset in PEERS:
            sum_copy(step, offset).start()

    pltpu.make_async_copy(right_got, right_got, right_send_sem).wait()
    pltpu.make_async_copy(sums, sums, sum_send_sem).wait()
    pltpu.make_async_copy(sums, sums, sum_recv_sem).wait()
    for step in range(ROUNDS):
        total = tiles[step, seq] + bias[...]
        for offset in range(1, seq_devices):
            total = total + sums[step, offset - 1]
        out_ref[step] = total


def on_device(features, gain, left_weight, right_weight, weight, bias):
    local_seqs, residues, channels = features.shape
    rows = local_seqs * residues
    f32, bf16 = jnp.float32, jnp.bfloat16
    dma = pltpu.SemaphoreType.DMA
    out = pl.pallas_call(
        kernel,
        out_shape=pltpu.VMEM((ROUNDS, 8, 128), f32),
        in_specs=[pl.BlockSpec(memory_space=pltpu.HBM)] * 6,
        out_specs=pl.BlockSpec(memory_space=pltpu.VMEM),
        scratch_shapes=[
            pltpu.VMEM((rows, channels), f32),
            pltpu.VMEM((1, channels), f32),
            pltpu.VMEM((32, channels), f32),
            pltpu.VMEM((32, channels), f32),
            pltpu.VMEM((1024, 128), f32),
            pltpu.VMEM((1, 128), f32),
            dma((6,)),
            pltpu.VMEM((256, channels), bf16),
            pltpu.VMEM((256, channels), bf16),
            pltpu.VMEM((1024, 256), bf16),
            pltpu.VMEM((rows, 128), f32),
            pltpu.VMEM((rows, 128), f32),
            pltpu.VMEM((256, 128), f32),
            pltpu.VMEM((256, 256), bf16),
            pltpu.VMEM((local_seqs, 256), f32),
            pltpu.VMEM((ROUNDS, local_seqs, 256), f32),
            pltpu.VMEM((256, 256), f32),
            pltpu.VMEM((ROUNDS, 8, 8, 128), f32),
            pltpu.VMEM((ROUNDS, 7, 8, 128), f32),
            dma,
            dma((ROUNDS,)),
            dma,
            dma,
        ],
        compiler_params=pltpu.CompilerParams(
            collective_id=0, has_side_effects=True, vmem_limit_bytes=32 * 1024 * 1024
        ),
    )(
        *(
            pltpu.with_memory_space_constraint(operand, pltpu.HBM)
            for operand in (
                features.reshape(rows, channels),
                gain.reshape(1, channels),
                left_weight.T,
                right_weight.T,
                weight,
                bias.reshape(1, 128),
            )
        )
    )
    return out.reshape(ROUNDS, 8, 1, 128)


def solution(mesh):
    in_specs = (P("seq", "res", None), P(), P(), P(), P(), P())
    out_specs = P(None, "res", "seq", None)
    return jax.shard_map(
        on_device, mesh=mesh, in_specs=in_specs, out_specs=out_specs, check_vma=False
    )
```

```python
import jax
import jax.numpy as jnp
from jax import lax
from jax.experimental import pallas as pl
from jax.experimental.pallas import tpu as pltpu
from jax.sharding import PartitionSpec as P

ROUNDS = 4
SEND_ORDER = (3, 2, 1, 0)
ROUND_ORDER = (3, 2, 1, 0)
MASKS = (1, 2, 6, 8)
HELD = (0, 1, 1, 3)
FAR = 2
SUMS = 29
NEAR_SLOT = (0, 1, None, 2)
PEERS = (6, 7, 4, 5, 2, 3, 1)


def split(value):
    high = value.astype(jnp.bfloat16)
    low = (value - high.astype(jnp.float32)).astype(jnp.bfloat16)
    return high, low


def matmul(a, b):
    return lax.dot_general(a, b, (((1,), (0,)), ((), ())), preferred_element_type=jnp.float32)


def matmul_nt(a, b):
    return lax.dot_general(a, b, (((1,), (1,)), ((), ())), preferred_element_type=jnp.float32)


def group_index(rows, width):
    return lax.broadcasted_iota(jnp.int32, (rows, 128), 1) // width


def pick(parts, group):
    result = parts[-1]
    for index in range(len(parts) - 2, -1, -1):
        result = jnp.where(group == index, parts[index], result)
    return result


def kernel(
    features_hbm,
    gain_hbm,
    left_hbm,
    right_hbm,
    weight_hbm,
    bias_hbm,
    out_ref,
    features,
    gain,
    left_weight,
    right_weight,
    weight,
    bias,
    in_sem,
    proj_high,
    proj_low,
    weight_split,
    left_rows,
    right_rows,
    left_turned,
    left_parts,
    left_mine,
    right_mine,
    right_got,
    outer,
    tiles,
    sums,
    right_send_sem,
    right_recv_sem,
    sum_send_sem,
    sum_recv_sem,
):
    rows = features.shape[0]
    local_seqs = rows // 8
    hidden = 32
    seq_devices = 8
    total_seqs = local_seqs * seq_devices

    block = lax.axis_index("res")
    seq = lax.axis_index("seq")

    def flip(index, mask):
        result = index
        for bit in (1, 2, 4, 8):
            if mask & bit:
                result = result + bit - 2 * bit * ((index // bit) % 2)
        return result

    def partner(step):
        return flip(block, MASKS[step])

    def peer(offset):
        return flip(seq, offset)

    def sum_peers(step):
        return PEERS + (0,) if step == FAR else PEERS

    copies = [
        pltpu.make_async_copy(source, target, in_sem.at[index])
        for index, (source, target) in enumerate(
            (
                (features_hbm, features),
                (left_hbm, left_weight),
                (right_hbm, right_weight),
                (gain_hbm, gain),
                (weight_hbm, weight),
                (bias_hbm, bias),
            )
        )
    ]
    for copy in copies:
        copy.start()

    barrier = pltpu.get_barrier_semaphore()
    for step in range(ROUNDS):
        pl.semaphore_signal(barrier, inc=1, device_id=(partner(step), seq))
    for offset in PEERS:
        pl.semaphore_signal(barrier, inc=1, device_id=(partner(FAR), peer(offset)))
        pl.semaphore_signal(barrier, inc=1, device_id=(block, peer(offset)))

    for copy in copies[1:4]:
        copy.wait()
    left_high, left_low = split(left_weight[...] * gain[...])
    right_high, right_low = split(right_weight[...] * gain[...])
    proj_high[...] = jnp.concatenate([left_high] * 4 + [right_high] * 4, axis=0)
    proj_low[...] = jnp.concatenate([left_low] * 4 + [right_low] * 4, axis=0)

    def right_copy(step):
        return pltpu.make_async_remote_copy(
            src_ref=left_mine if step == FAR else right_mine,
            dst_ref=right_got.at[step],
            send_sem=right_send_sem,
            recv_sem=right_recv_sem.at[step],
            device_id=(partner(step), seq),
        )

    copies[0].wait()
    values = features[...]
    centered = values - jnp.mean(values, axis=1, keepdims=True)
    variance = jnp.mean(centered * centered, axis=1, keepdims=True)
    high, low = split(centered * lax.rsqrt(variance + 1e-05))
    projected = (
        matmul_nt(high, proj_low[...]) + matmul_nt(low, proj_high[...])
    ) + matmul_nt(high, proj_high[...])
    left_rows[...] = projected[:, :128]
    right_rows[...] = projected[:, 128:]
    seq_group = group_index(local_seqs, hidden)
    for source, target, scale in (
        (left_rows, left_mine, 1.0 / total_seqs),
        (right_rows, right_mine, 1.0),
    ):
        for half in range(2):
            lanes = [source[pl.ds(half * 4 + x, local_seqs, stride=8), :] for x in range(4)]
            target[:, pl.ds(half * 128, 128)] = pick(lanes, seq_group) * scale
    pl.semaphore_wait(barrier, ROUNDS + 2 * (seq_devices - 1))
    for step in SEND_ORDER:
        right_copy(step).start()

    def turn_left(rows):
        for half in range(2):
            left_half = rows[:, half * 128 : half * 128 + 128]
            left_turned[pl.ds(half * 128, 128), :] = jnp.concatenate(
                [left_half, left_half], axis=0
            ).T
        left_columns = jnp.concatenate(
            [left_turned[pl.ds(c, 8, stride=hidden), :] for c in range(hidden)], axis=0
        )
        turned_high, turned_low = split(left_columns)
        return jnp.concatenate([turned_high, turned_low], axis=1)

    left_parts[...] = turn_left(left_mine[...])

    for copy in copies[4:]:
        copy.wait()
    weight_high, weight_low = split(weight[...])
    weight_split[...] = jnp.concatenate([weight_high, weight_low], axis=1)

    def sum_slot(step, offset):
        if step == FAR:
            return SUMS - seq_devices + offset
        return NEAR_SLOT[step] * (seq_devices - 1) + offset - 1

    def sum_copy(step, offset):
        return pltpu.make_async_remote_copy(
            src_ref=tiles.at[step, peer(offset)],
            dst_ref=sums.at[sum_slot(step, offset)],
            send_sem=sum_send_sem,
            recv_sem=sum_recv_sem,
            device_id=(partner(FAR) if step == FAR else block, peer(offset)),
        )

    group = group_index(8, hidden)
    for step in ROUND_ORDER:
        if step != HELD[FAR]:
            right_copy(step).wait_recv()
        if step == FAR:
            left = turn_left(right_got[FAR])
            right_copy(HELD[FAR]).wait_recv()
        else:
            left = left_parts[...]
        right_high, right_low = split(right_got[HELD[step]])
        outer[...] = matmul(
            left,
            jnp.concatenate([right_high, right_low, right_high, right_low], axis=0),
        )
        pieces = []
        for y_half in range(2):
            columns = [[None] * 8 for _ in range(4)]
            for c_quad in range(8):
                turned = [
                    outer[pl.ds((c_quad * 4 + i) * 8, 8), pl.ds(y_half * 128, 128)]
                    for i in range(4)
                ]
                turned = [turned[0]] + [pltpu.roll(turned[i], 32 * i, 1) for i in range(1, 4)]
                for y in range(4):
                    mixed = pick([turned[(g - y) % 4] for g in range(4)], group)
                    if y:
                        mixed = pltpu.roll(mixed, 128 - 32 * y, 1)
                    columns[y][c_quad] = mixed
            for y in range(4):
                pieces.append(jnp.concatenate(columns[y], axis=1))
        flat_high, flat_low = split(jnp.concatenate(pieces, axis=0))
        product = matmul(jnp.concatenate([flat_high, flat_low], axis=0), weight_split[...])
        total = (product[64:, 128:] + product[64:, :128]) + (product[:64, 128:] + product[:64, :128])
        tiles[step] = total.reshape(8, 8, 128)
        for offset in sum_peers(step):
            sum_copy(step, offset).start()

    pltpu.make_async_copy(right_got, right_got, right_send_sem).wait()
    pltpu.make_async_copy(sums, sums, sum_send_sem).wait()
    pltpu.make_async_copy(sums, sums, sum_recv_sem).wait()
    for step in range(ROUNDS):
        total = bias[...] if step == FAR else tiles[step, seq] + bias[...]
        for offset in sum_peers(step):
            total = total + sums[sum_slot(step, offset)]
        out_ref[step] = total


def on_device(features, gain, left_weight, right_weight, weight, bias):
    local_seqs, residues, channels = features.shape
    rows = local_seqs * residues
    f32, bf16 = jnp.float32, jnp.bfloat16
    dma = pltpu.SemaphoreType.DMA
    out = pl.pallas_call(
        kernel,
        out_shape=pltpu.VMEM((ROUNDS, 8, 128), f32),
        in_specs=[pl.BlockSpec(memory_space=pltpu.HBM)] * 6,
        out_specs=pl.BlockSpec(memory_space=pltpu.VMEM),
        scratch_shapes=[
            pltpu.VMEM((rows, channels), f32),
            pltpu.VMEM((1, channels), f32),
            pltpu.VMEM((32, channels), f32),
            pltpu.VMEM((32, channels), f32),
            pltpu.VMEM((1024, 128), f32),
            pltpu.VMEM((1, 128), f32),
            dma((6,)),
            pltpu.VMEM((256, channels), bf16),
            pltpu.VMEM((256, channels), bf16),
            pltpu.VMEM((1024, 256), bf16),
            pltpu.VMEM((rows, 128), f32),
            pltpu.VMEM((rows, 128), f32),
            pltpu.VMEM((256, 128), f32),
            pltpu.VMEM((256, 256), bf16),
            pltpu.VMEM((local_seqs, 256), f32),
            pltpu.VMEM((local_seqs, 256), f32),
            pltpu.VMEM((ROUNDS, local_seqs, 256), f32),
            pltpu.VMEM((256, 256), f32),
            pltpu.VMEM((ROUNDS, 8, 8, 128), f32),
            pltpu.VMEM((SUMS, 8, 128), f32),
            dma,
            dma((ROUNDS,)),
            dma,
            dma,
        ],
        compiler_params=pltpu.CompilerParams(
            collective_id=0, has_side_effects=True, vmem_limit_bytes=32 * 1024 * 1024
        ),
    )(
        *(
            pltpu.with_memory_space_constraint(operand, pltpu.HBM)
            for operand in (
                features.reshape(rows, channels),
                gain.reshape(1, channels),
                left_weight.T,
                right_weight.T,
                weight,
                bias.reshape(1, 128),
            )
        )
    )
    return out.reshape(ROUNDS, 8, 1, 128)


def solution(mesh):
    in_specs = (P("seq", "res", None), P(), P(), P(), P(), P())
    out_specs = P(None, "res", "seq", None)
    return jax.shard_map(
        on_device, mesh=mesh, in_specs=in_specs, out_specs=out_specs, check_vma=False
    )
```

```python
import jax
import jax.numpy as jnp
from jax import lax
from jax.experimental import pallas as pl
from jax.experimental.pallas import tpu as pltpu
from jax.sharding import PartitionSpec as P

ROUNDS = 4
SEND_ORDER = (3, 2, 1, 0)
ROUND_ORDER = (3, 2, 1, 0)
MASKS = (1, 2, 6, 8)
HELD = (0, 1, 1, 3)
FAR = 2
SUMS = 29
NEAR_SLOT = (0, 1, None, 2)
PEERS = (6, 7, 4, 5, 2, 3, 1)
GREETED = (4, 5, 2, 3, 1)


def split(value):
    high = value.astype(jnp.bfloat16)
    low = (value - high.astype(jnp.float32)).astype(jnp.bfloat16)
    return high, low


def matmul(a, b):
    return lax.dot_general(a, b, (((1,), (0,)), ((), ())), preferred_element_type=jnp.float32)


def matmul_nt(a, b):
    return lax.dot_general(a, b, (((1,), (1,)), ((), ())), preferred_element_type=jnp.float32)


def group_index(rows, width):
    return lax.broadcasted_iota(jnp.int32, (rows, 128), 1) // width


def pick(parts, group):
    result = parts[-1]
    for index in range(len(parts) - 2, -1, -1):
        result = jnp.where(group == index, parts[index], result)
    return result


def kernel(
    features_hbm,
    gain_hbm,
    left_hbm,
    right_hbm,
    weight_hbm,
    bias_hbm,
    out_ref,
    features,
    gain,
    left_weight,
    right_weight,
    weight,
    bias,
    in_sem,
    proj_high,
    proj_low,
    weight_split,
    left_rows,
    right_rows,
    left_turned,
    left_parts,
    left_mine,
    right_mine,
    right_got,
    outer,
    tiles,
    sums,
    right_send_sem,
    right_recv_sem,
    sum_send_sem,
    sum_recv_sem,
    peers_ready,
    far_ready,
):
    rows = features.shape[0]
    local_seqs = rows // 8
    hidden = 32
    seq_devices = 8
    total_seqs = local_seqs * seq_devices

    block = lax.axis_index("res")
    seq = lax.axis_index("seq")

    def flip(index, mask):
        result = index
        for bit in (1, 2, 4, 8):
            if mask & bit:
                result = result + bit - 2 * bit * ((index // bit) % 2)
        return result

    def partner(step):
        return flip(block, MASKS[step])

    def peer(offset):
        return flip(seq, offset)

    def sum_peers(step):
        return PEERS + (0,) if step == FAR else PEERS

    copies = [
        pltpu.make_async_copy(source, target, in_sem.at[index])
        for index, (source, target) in enumerate(
            (
                (features_hbm, features),
                (left_hbm, left_weight),
                (right_hbm, right_weight),
                (gain_hbm, gain),
                (weight_hbm, weight),
                (bias_hbm, bias),
            )
        )
    ]
    for copy in copies:
        copy.start()

    barrier = pltpu.get_barrier_semaphore()
    for step in range(ROUNDS):
        pl.semaphore_signal(barrier, inc=1, device_id=(partner(step), seq))
    for offset in GREETED:
        pl.semaphore_signal(barrier, inc=1, device_id=(block, peer(offset)))

    for copy in copies[1:4]:
        copy.wait()
    left_high, left_low = split(left_weight[...] * gain[...])
    right_high, right_low = split(right_weight[...] * gain[...])
    proj_high[...] = jnp.concatenate([left_high] * 4 + [right_high] * 4, axis=0)
    proj_low[...] = jnp.concatenate([left_low] * 4 + [right_low] * 4, axis=0)

    def right_copy(step):
        return pltpu.make_async_remote_copy(
            src_ref=left_mine if step == FAR else right_mine,
            dst_ref=right_got.at[step],
            send_sem=right_send_sem,
            recv_sem=right_recv_sem.at[step],
            device_id=(partner(step), seq),
        )

    copies[0].wait()
    values = features[...]
    centered = values - jnp.mean(values, axis=1, keepdims=True)
    variance = jnp.mean(centered * centered, axis=1, keepdims=True)
    high, low = split(centered * lax.rsqrt(variance + 1e-05))
    projected = (
        matmul_nt(high, proj_low[...]) + matmul_nt(low, proj_high[...])
    ) + matmul_nt(high, proj_high[...])
    left_rows[...] = projected[:, :128]
    right_rows[...] = projected[:, 128:]
    seq_group = group_index(local_seqs, hidden)
    for source, target, scale in (
        (left_rows, left_mine, 1.0 / total_seqs),
        (right_rows, right_mine, 1.0),
    ):
        for half in range(2):
            lanes = [source[pl.ds(half * 4 + x, local_seqs, stride=8), :] for x in range(4)]
            target[:, pl.ds(half * 128, 128)] = pick(lanes, seq_group) * scale
    pl.semaphore_wait(barrier, ROUNDS + len(GREETED))
    for step in SEND_ORDER:
        right_copy(step).start()
    for offset in GREETED:
        pl.semaphore_signal(peers_ready, inc=1, device_id=(block, peer(offset)))

    def turn_left(rows):
        for half in range(2):
            left_half = rows[:, half * 128 : half * 128 + 128]
            left_turned[pl.ds(half * 128, 128), :] = jnp.concatenate(
                [left_half, left_half], axis=0
            ).T
        left_columns = jnp.concatenate(
            [left_turned[pl.ds(c, 8, stride=hidden), :] for c in range(hidden)], axis=0
        )
        turned_high, turned_low = split(left_columns)
        return jnp.concatenate([turned_high, turned_low], axis=1)

    left_parts[...] = turn_left(left_mine[...])

    for copy in copies[4:]:
        copy.wait()
    weight_high, weight_low = split(weight[...])
    weight_split[...] = jnp.concatenate([weight_high, weight_low], axis=1)

    pl.semaphore_wait(peers_ready, len(GREETED))
    pl.semaphore_signal(far_ready, inc=1, device_id=(partner(FAR), seq))

    def sum_slot(step, offset):
        if step == FAR:
            return SUMS - seq_devices + offset
        return NEAR_SLOT[step] * (seq_devices - 1) + offset - 1

    def sum_copy(step, offset):
        return pltpu.make_async_remote_copy(
            src_ref=tiles.at[step, peer(offset)],
            dst_ref=sums.at[sum_slot(step, offset)],
            send_sem=sum_send_sem,
            recv_sem=sum_recv_sem,
            device_id=(partner(FAR) if step == FAR else block, peer(offset)),
        )

    group = group_index(8, hidden)
    for step in ROUND_ORDER:
        if step != HELD[FAR]:
            right_copy(step).wait_recv()
        if step == FAR:
            left = turn_left(right_got[FAR])
            right_copy(HELD[FAR]).wait_recv()
        else:
            left = left_parts[...]
        right_high, right_low = split(right_got[HELD[step]])
        outer[...] = matmul(
            left,
            jnp.concatenate([right_high, right_low, right_high, right_low], axis=0),
        )
        pieces = []
        for y_half in range(2):
            columns = [[None] * 8 for _ in range(4)]
            for c_quad in range(8):
                turned = [
                    outer[pl.ds((c_quad * 4 + i) * 8, 8), pl.ds(y_half * 128, 128)]
                    for i in range(4)
                ]
                turned = [turned[0]] + [pltpu.roll(turned[i], 32 * i, 1) for i in range(1, 4)]
                for y in range(4):
                    mixed = pick([turned[(g - y) % 4] for g in range(4)], group)
                    if y:
                        mixed = pltpu.roll(mixed, 128 - 32 * y, 1)
                    columns[y][c_quad] = mixed
            for y in range(4):
                pieces.append(jnp.concatenate(columns[y], axis=1))
        flat_high, flat_low = split(jnp.concatenate(pieces, axis=0))
        product = matmul(jnp.concatenate([flat_high, flat_low], axis=0), weight_split[...])
        total = (product[64:, 128:] + product[64:, :128]) + (product[:64, 128:] + product[:64, :128])
        tiles[step] = total.reshape(8, 8, 128)
        if step == FAR:
            pl.semaphore_wait(far_ready, 1)
        for offset in sum_peers(step):
            sum_copy(step, offset).start()

    pltpu.make_async_copy(right_got, right_got, right_send_sem).wait()
    pltpu.make_async_copy(sums, sums, sum_send_sem).wait()
    pltpu.make_async_copy(sums, sums, sum_recv_sem).wait()
    for step in range(ROUNDS):
        total = bias[...] if step == FAR else tiles[step, seq] + bias[...]
        for offset in sum_peers(step):
            total = total + sums[sum_slot(step, offset)]
        out_ref[step] = total


def on_device(features, gain, left_weight, right_weight, weight, bias):
    local_seqs, residues, channels = features.shape
    rows = local_seqs * residues
    f32, bf16 = jnp.float32, jnp.bfloat16
    dma = pltpu.SemaphoreType.DMA
    out = pl.pallas_call(
        kernel,
        out_shape=pltpu.VMEM((ROUNDS, 8, 128), f32),
        in_specs=[pl.BlockSpec(memory_space=pltpu.HBM)] * 6,
        out_specs=pl.BlockSpec(memory_space=pltpu.VMEM),
        scratch_shapes=[
            pltpu.VMEM((rows, channels), f32),
            pltpu.VMEM((1, channels), f32),
            pltpu.VMEM((32, channels), f32),
            pltpu.VMEM((32, channels), f32),
            pltpu.VMEM((1024, 128), f32),
            pltpu.VMEM((1, 128), f32),
            dma((6,)),
            pltpu.VMEM((256, channels), bf16),
            pltpu.VMEM((256, channels), bf16),
            pltpu.VMEM((1024, 256), bf16),
            pltpu.VMEM((rows, 128), f32),
            pltpu.VMEM((rows, 128), f32),
            pltpu.VMEM((256, 128), f32),
            pltpu.VMEM((256, 256), bf16),
            pltpu.VMEM((local_seqs, 256), f32),
            pltpu.VMEM((local_seqs, 256), f32),
            pltpu.VMEM((ROUNDS, local_seqs, 256), f32),
            pltpu.VMEM((256, 256), f32),
            pltpu.VMEM((ROUNDS, 8, 8, 128), f32),
            pltpu.VMEM((SUMS, 8, 128), f32),
            dma,
            dma((ROUNDS,)),
            dma,
            dma,
            pltpu.SemaphoreType.REGULAR,
            pltpu.SemaphoreType.REGULAR,
        ],
        compiler_params=pltpu.CompilerParams(
            collective_id=0, has_side_effects=True, vmem_limit_bytes=32 * 1024 * 1024
        ),
    )(
        *(
            pltpu.with_memory_space_constraint(operand, pltpu.HBM)
            for operand in (
                features.reshape(rows, channels),
                gain.reshape(1, channels),
                left_weight.T,
                right_weight.T,
                weight,
                bias.reshape(1, 128),
            )
        )
    )
    return out.reshape(ROUNDS, 8, 1, 128)


def solution(mesh):
    in_specs = (P("seq", "res", None), P(), P(), P(), P(), P())
    out_specs = P(None, "res", "seq", None)
    return jax.shard_map(
        on_device, mesh=mesh, in_specs=in_specs, out_specs=out_specs, check_vma=False
    )
```

```python
import jax
import jax.numpy as jnp
from jax import lax
from jax.experimental import pallas as pl
from jax.experimental.pallas import tpu as pltpu
from jax.sharding import PartitionSpec as P

ROUNDS = 4
EARLY_SENDS = (3, 2, 1, 0)
LATE_SENDS = (3, 1, 2, 0)
EARLY_ROUNDS = (1, 0, 2)
LATE_ROUNDS = (2, 1, 0)
MASKS = (1, 2, 6, 8)
HELD = (0, 1, 1, 3)
FAR = 2
SUMS = 29
NEAR_SLOT = (0, 1, None, 2)
PEERS = (6, 7, 4, 5, 2, 3, 1)
GREETED = (4, 5, 2, 3, 1)


def split(value):
    high = value.astype(jnp.bfloat16)
    low = (value - high.astype(jnp.float32)).astype(jnp.bfloat16)
    return high, low


def matmul(a, b):
    return lax.dot_general(a, b, (((1,), (0,)), ((), ())), preferred_element_type=jnp.float32)


def matmul_nt(a, b):
    return lax.dot_general(a, b, (((1,), (1,)), ((), ())), preferred_element_type=jnp.float32)


def group_index(rows, width):
    return lax.broadcasted_iota(jnp.int32, (rows, 128), 1) // width


def pick(parts, group):
    result = parts[-1]
    for index in range(len(parts) - 2, -1, -1):
        result = jnp.where(group == index, parts[index], result)
    return result


def kernel(
    features_hbm,
    gain_hbm,
    left_hbm,
    right_hbm,
    weight_hbm,
    bias_hbm,
    out_ref,
    features,
    gain,
    left_weight,
    right_weight,
    weight,
    bias,
    in_sem,
    proj_high,
    proj_low,
    weight_split,
    left_rows,
    right_rows,
    left_turned,
    left_parts,
    left_mine,
    right_mine,
    right_got,
    outer,
    tiles,
    sums,
    right_send_sem,
    right_recv_sem,
    sum_send_sem,
    sum_recv_sem,
    peers_ready,
    far_ready,
):
    rows = features.shape[0]
    local_seqs = rows // 8
    hidden = 32
    seq_devices = 8
    total_seqs = local_seqs * seq_devices

    block = lax.axis_index("res")
    seq = lax.axis_index("seq")

    def flip(index, mask):
        result = index
        for bit in (1, 2, 4, 8):
            if mask & bit:
                result = result + bit - 2 * bit * ((index // bit) % 2)
        return result

    def partner(step):
        return flip(block, MASKS[step])

    def peer(offset):
        return flip(seq, offset)

    def sum_peers(step):
        return PEERS + (0,) if step == FAR else PEERS

    copies = [
        pltpu.make_async_copy(source, target, in_sem.at[index])
        for index, (source, target) in enumerate(
            (
                (features_hbm, features),
                (left_hbm, left_weight),
                (right_hbm, right_weight),
                (gain_hbm, gain),
                (weight_hbm, weight),
                (bias_hbm, bias),
            )
        )
    ]
    for copy in copies:
        copy.start()

    barrier = pltpu.get_barrier_semaphore()
    for step in range(ROUNDS):
        pl.semaphore_signal(barrier, inc=1, device_id=(partner(step), seq))
    for offset in GREETED:
        pl.semaphore_signal(barrier, inc=1, device_id=(block, peer(offset)))

    for copy in copies[1:4]:
        copy.wait()
    left_high, left_low = split(left_weight[...] * gain[...])
    right_high, right_low = split(right_weight[...] * gain[...])
    proj_high[...] = jnp.concatenate([left_high] * 4 + [right_high] * 4, axis=0)
    proj_low[...] = jnp.concatenate([left_low] * 4 + [right_low] * 4, axis=0)

    def right_copy(step):
        return pltpu.make_async_remote_copy(
            src_ref=left_mine if step == FAR else right_mine,
            dst_ref=right_got.at[step],
            send_sem=right_send_sem,
            recv_sem=right_recv_sem.at[step],
            device_id=(partner(step), seq),
        )

    copies[0].wait()
    values = features[...]
    centered = values - jnp.mean(values, axis=1, keepdims=True)
    variance = jnp.mean(centered * centered, axis=1, keepdims=True)
    high, low = split(centered * lax.rsqrt(variance + 1e-05))
    projected = (
        matmul_nt(high, proj_low[...]) + matmul_nt(low, proj_high[...])
    ) + matmul_nt(high, proj_high[...])
    left_rows[...] = projected[:, :128]
    right_rows[...] = projected[:, 128:]
    seq_group = group_index(local_seqs, hidden)
    for source, target, scale in (
        (left_rows, left_mine, 1.0 / total_seqs),
        (right_rows, right_mine, 1.0),
    ):
        for half in range(2):
            lanes = [source[pl.ds(half * 4 + x, local_seqs, stride=8), :] for x in range(4)]
            target[:, pl.ds(half * 128, 128)] = pick(lanes, seq_group) * scale
    pl.semaphore_wait(barrier, ROUNDS + len(GREETED))
    early = block % 8 < 4

    @pl.when(early)
    def _():
        for step in EARLY_SENDS:
            right_copy(step).start()

    @pl.when(jnp.logical_not(early))
    def _():
        for step in LATE_SENDS:
            right_copy(step).start()

    for offset in GREETED:
        pl.semaphore_signal(peers_ready, inc=1, device_id=(block, peer(offset)))

    def turn_left(rows):
        for half in range(2):
            left_half = rows[:, half * 128 : half * 128 + 128]
            left_turned[pl.ds(half * 128, 128), :] = jnp.concatenate(
                [left_half, left_half], axis=0
            ).T
        left_columns = jnp.concatenate(
            [left_turned[pl.ds(c, 8, stride=hidden), :] for c in range(hidden)], axis=0
        )
        turned_high, turned_low = split(left_columns)
        return jnp.concatenate([turned_high, turned_low], axis=1)

    left_parts[...] = turn_left(left_mine[...])

    for copy in copies[4:]:
        copy.wait()
    weight_high, weight_low = split(weight[...])
    weight_split[...] = jnp.concatenate([weight_high, weight_low], axis=1)

    pl.semaphore_wait(peers_ready, len(GREETED))
    pl.semaphore_signal(far_ready, inc=1, device_id=(partner(FAR), seq))

    def sum_slot(step, offset):
        if step == FAR:
            return SUMS - seq_devices + offset
        return NEAR_SLOT[step] * (seq_devices - 1) + offset - 1

    def sum_copy(step, offset):
        return pltpu.make_async_remote_copy(
            src_ref=tiles.at[step, peer(offset)],
            dst_ref=sums.at[sum_slot(step, offset)],
            send_sem=sum_send_sem,
            recv_sem=sum_recv_sem,
            device_id=(partner(FAR) if step == FAR else block, peer(offset)),
        )

    group = group_index(8, hidden)
    def compute_round(step, arrived):
        if step not in arrived:
            right_copy(step).wait_recv()
        if step == FAR:
            left = turn_left(right_got[FAR])
            if HELD[FAR] not in arrived:
                right_copy(HELD[FAR]).wait_recv()
        else:
            left = left_parts[...]
        right_high, right_low = split(right_got[HELD[step]])
        outer[...] = matmul(
            left,
            jnp.concatenate([right_high, right_low, right_high, right_low], axis=0),
        )
        pieces = []
        for y_half in range(2):
            columns = [[None] * 8 for _ in range(4)]
            for c_quad in range(8):
                turned = [
                    outer[pl.ds((c_quad * 4 + i) * 8, 8), pl.ds(y_half * 128, 128)]
                    for i in range(4)
                ]
                turned = [turned[0]] + [pltpu.roll(turned[i], 32 * i, 1) for i in range(1, 4)]
                for y in range(4):
                    mixed = pick([turned[(g - y) % 4] for g in range(4)], group)
                    if y:
                        mixed = pltpu.roll(mixed, 128 - 32 * y, 1)
                    columns[y][c_quad] = mixed
            for y in range(4):
                pieces.append(jnp.concatenate(columns[y], axis=1))
        flat_high, flat_low = split(jnp.concatenate(pieces, axis=0))
        product = matmul(jnp.concatenate([flat_high, flat_low], axis=0), weight_split[...])
        total = (product[64:, 128:] + product[64:, :128]) + (product[:64, 128:] + product[:64, :128])
        tiles[step] = total.reshape(8, 8, 128)
        if step == FAR:
            pl.semaphore_wait(far_ready, 1)
        for offset in sum_peers(step):
            sum_copy(step, offset).start()

    compute_round(3, ())

    @pl.when(early)
    def _():
        for index, step in enumerate(EARLY_ROUNDS):
            compute_round(step, EARLY_ROUNDS[:index])

    @pl.when(jnp.logical_not(early))
    def _():
        for index, step in enumerate(LATE_ROUNDS):
            compute_round(step, (HELD[FAR],) if index else ())

    pltpu.make_async_copy(right_got, right_got, right_send_sem).wait()
    pltpu.make_async_copy(sums, sums, sum_send_sem).wait()
    pltpu.make_async_copy(sums, sums, sum_recv_sem).wait()
    for step in range(ROUNDS):
        total = bias[...] if step == FAR else tiles[step, seq] + bias[...]
        for offset in sum_peers(step):
            total = total + sums[sum_slot(step, offset)]
        out_ref[step] = total


def on_device(features, gain, left_weight, right_weight, weight, bias):
    local_seqs, residues, channels = features.shape
    rows = local_seqs * residues
    f32, bf16 = jnp.float32, jnp.bfloat16
    dma = pltpu.SemaphoreType.DMA
    out = pl.pallas_call(
        kernel,
        out_shape=pltpu.VMEM((ROUNDS, 8, 128), f32),
        in_specs=[pl.BlockSpec(memory_space=pltpu.HBM)] * 6,
        out_specs=pl.BlockSpec(memory_space=pltpu.VMEM),
        scratch_shapes=[
            pltpu.VMEM((rows, channels), f32),
            pltpu.VMEM((1, channels), f32),
            pltpu.VMEM((32, channels), f32),
            pltpu.VMEM((32, channels), f32),
            pltpu.VMEM((1024, 128), f32),
            pltpu.VMEM((1, 128), f32),
            dma((6,)),
            pltpu.VMEM((256, channels), bf16),
            pltpu.VMEM((256, channels), bf16),
            pltpu.VMEM((1024, 256), bf16),
            pltpu.VMEM((rows, 128), f32),
            pltpu.VMEM((rows, 128), f32),
            pltpu.VMEM((256, 128), f32),
            pltpu.VMEM((256, 256), bf16),
            pltpu.VMEM((local_seqs, 256), f32),
            pltpu.VMEM((local_seqs, 256), f32),
            pltpu.VMEM((ROUNDS, local_seqs, 256), f32),
            pltpu.VMEM((256, 256), f32),
            pltpu.VMEM((ROUNDS, 8, 8, 128), f32),
            pltpu.VMEM((SUMS, 8, 128), f32),
            dma,
            dma((ROUNDS,)),
            dma,
            dma,
            pltpu.SemaphoreType.REGULAR,
            pltpu.SemaphoreType.REGULAR,
        ],
        compiler_params=pltpu.CompilerParams(
            collective_id=0, has_side_effects=True, vmem_limit_bytes=32 * 1024 * 1024
        ),
    )(
        *(
            pltpu.with_memory_space_constraint(operand, pltpu.HBM)
            for operand in (
                features.reshape(rows, channels),
                gain.reshape(1, channels),
                left_weight.T,
                right_weight.T,
                weight,
                bias.reshape(1, 128),
            )
        )
    )
    return out.reshape(ROUNDS, 8, 1, 128)


def solution(mesh):
    in_specs = (P("seq", "res", None), P(), P(), P(), P(), P())
    out_specs = P(None, "res", "seq", None)
    return jax.shard_map(
        on_device, mesh=mesh, in_specs=in_specs, out_specs=out_specs, check_vma=False
    )
```

```python
import jax
import jax.numpy as jnp
from jax import lax
from jax.experimental import pallas as pl
from jax.experimental.pallas import tpu as pltpu
from jax.sharding import PartitionSpec as P

ROUNDS = 4
EARLY_SENDS = (3, 2, 1, 0)
LATE_SENDS = (3, 1, 2, 0)
EARLY_ROUNDS = (0, 1, 3, 2)
LATE_ROUNDS = (2, 3, 1, 0)
MASKS = (1, 2, 6, 8)
HELD = (0, 1, 1, 3)
FAR = 2
SUMS = 29
NEAR_SLOT = (0, 1, None, 2)
PEERS = (6, 7, 4, 5, 2, 3, 1)
GREETED = (4, 5, 2, 3, 1)


def split(value):
    high = value.astype(jnp.bfloat16)
    low = (value - high.astype(jnp.float32)).astype(jnp.bfloat16)
    return high, low


def matmul(a, b):
    return lax.dot_general(a, b, (((1,), (0,)), ((), ())), preferred_element_type=jnp.float32)


def matmul_nt(a, b):
    return lax.dot_general(a, b, (((1,), (1,)), ((), ())), preferred_element_type=jnp.float32)


def group_index(rows, width):
    return lax.broadcasted_iota(jnp.int32, (rows, 128), 1) // width


def pick(parts, group):
    result = parts[-1]
    for index in range(len(parts) - 2, -1, -1):
        result = jnp.where(group == index, parts[index], result)
    return result


def kernel(
    features_hbm,
    gain_hbm,
    left_hbm,
    right_hbm,
    weight_hbm,
    bias_hbm,
    out_ref,
    features,
    gain,
    left_weight,
    right_weight,
    weight,
    bias,
    in_sem,
    proj_high,
    proj_low,
    weight_split,
    left_rows,
    right_rows,
    left_turned,
    left_parts,
    left_mine,
    right_mine,
    right_got,
    outer,
    tiles,
    sums,
    right_send_sem,
    right_recv_sem,
    sum_send_sem,
    sum_recv_sem,
    peers_ready,
    far_ready,
):
    rows = features.shape[0]
    local_seqs = rows // 8
    hidden = 32
    seq_devices = 8
    total_seqs = local_seqs * seq_devices

    block = lax.axis_index("res")
    seq = lax.axis_index("seq")

    def flip(index, mask):
        result = index
        for bit in (1, 2, 4, 8):
            if mask & bit:
                result = result + bit - 2 * bit * ((index // bit) % 2)
        return result

    def partner(step):
        return flip(block, MASKS[step])

    def peer(offset):
        return flip(seq, offset)

    def sum_peers(step):
        return PEERS + (0,) if step == FAR else PEERS

    copies = [
        pltpu.make_async_copy(source, target, in_sem.at[index])
        for index, (source, target) in enumerate(
            (
                (features_hbm, features),
                (left_hbm, left_weight),
                (right_hbm, right_weight),
                (gain_hbm, gain),
                (weight_hbm, weight),
                (bias_hbm, bias),
            )
        )
    ]
    for copy in copies:
        copy.start()

    barrier = pltpu.get_barrier_semaphore()
    for step in range(ROUNDS):
        pl.semaphore_signal(barrier, inc=1, device_id=(partner(step), seq))
    for offset in GREETED:
        pl.semaphore_signal(barrier, inc=1, device_id=(block, peer(offset)))

    for copy in copies[1:4]:
        copy.wait()
    left_high, left_low = split(left_weight[...] * gain[...])
    right_high, right_low = split(right_weight[...] * gain[...])
    proj_high[...] = jnp.concatenate([left_high] * 4 + [right_high] * 4, axis=0)
    proj_low[...] = jnp.concatenate([left_low] * 4 + [right_low] * 4, axis=0)

    def right_copy(step):
        return pltpu.make_async_remote_copy(
            src_ref=left_mine if step == FAR else right_mine,
            dst_ref=right_got.at[step],
            send_sem=right_send_sem,
            recv_sem=right_recv_sem.at[step],
            device_id=(partner(step), seq),
        )

    copies[0].wait()
    values = features[...]
    centered = values - jnp.mean(values, axis=1, keepdims=True)
    variance = jnp.mean(centered * centered, axis=1, keepdims=True)
    high, low = split(centered * lax.rsqrt(variance + 1e-05))
    projected = (
        matmul_nt(high, proj_low[...]) + matmul_nt(low, proj_high[...])
    ) + matmul_nt(high, proj_high[...])
    left_rows[...] = projected[:, :128]
    right_rows[...] = projected[:, 128:]
    seq_group = group_index(local_seqs, hidden)
    for source, target, scale in (
        (left_rows, left_mine, 1.0 / total_seqs),
        (right_rows, right_mine, 1.0),
    ):
        for half in range(2):
            lanes = [source[pl.ds(half * 4 + x, local_seqs, stride=8), :] for x in range(4)]
            target[:, pl.ds(half * 128, 128)] = pick(lanes, seq_group) * scale
    pl.semaphore_wait(barrier, ROUNDS + len(GREETED))
    early = block % 8 < 4

    @pl.when(early)
    def _():
        for step in EARLY_SENDS:
            right_copy(step).start()

    @pl.when(jnp.logical_not(early))
    def _():
        for step in LATE_SENDS:
            right_copy(step).start()

    for offset in GREETED:
        pl.semaphore_signal(peers_ready, inc=1, device_id=(block, peer(offset)))

    def turn_left(rows):
        for half in range(2):
            left_half = rows[:, half * 128 : half * 128 + 128]
            left_turned[pl.ds(half * 128, 128), :] = jnp.concatenate(
                [left_half, left_half], axis=0
            ).T
        left_columns = jnp.concatenate(
            [left_turned[pl.ds(c, 8, stride=hidden), :] for c in range(hidden)], axis=0
        )
        turned_high, turned_low = split(left_columns)
        return jnp.concatenate([turned_high, turned_low], axis=1)

    left_parts[...] = turn_left(left_mine[...])

    for copy in copies[4:]:
        copy.wait()
    weight_high, weight_low = split(weight[...])
    weight_split[...] = jnp.concatenate([weight_high, weight_low], axis=1)

    pl.semaphore_wait(peers_ready, len(GREETED))
    pl.semaphore_signal(far_ready, inc=1, device_id=(partner(FAR), seq))

    def sum_slot(step, offset):
        if step == FAR:
            return SUMS - seq_devices + offset
        return NEAR_SLOT[step] * (seq_devices - 1) + offset - 1

    def sum_copy(step, offset):
        return pltpu.make_async_remote_copy(
            src_ref=tiles.at[step, peer(offset)],
            dst_ref=sums.at[sum_slot(step, offset)],
            send_sem=sum_send_sem,
            recv_sem=sum_recv_sem,
            device_id=(partner(FAR) if step == FAR else block, peer(offset)),
        )

    group = group_index(8, hidden)
    def compute_round(step, arrived):
        if step not in arrived:
            right_copy(step).wait_recv()
        if step == FAR:
            left = turn_left(right_got[FAR])
            if HELD[FAR] not in arrived:
                right_copy(HELD[FAR]).wait_recv()
        else:
            left = left_parts[...]
        right_high, right_low = split(right_got[HELD[step]])
        outer[...] = matmul(
            left,
            jnp.concatenate([right_high, right_low, right_high, right_low], axis=0),
        )
        pieces = []
        for y_half in range(2):
            columns = [[None] * 8 for _ in range(4)]
            for c_quad in range(8):
                turned = [
                    outer[pl.ds((c_quad * 4 + i) * 8, 8), pl.ds(y_half * 128, 128)]
                    for i in range(4)
                ]
                turned = [turned[0]] + [pltpu.roll(turned[i], 32 * i, 1) for i in range(1, 4)]
                for y in range(4):
                    mixed = pick([turned[(g - y) % 4] for g in range(4)], group)
                    if y:
                        mixed = pltpu.roll(mixed, 128 - 32 * y, 1)
                    columns[y][c_quad] = mixed
            for y in range(4):
                pieces.append(jnp.concatenate(columns[y], axis=1))
        flat_high, flat_low = split(jnp.concatenate(pieces, axis=0))
        product = matmul(jnp.concatenate([flat_high, flat_low], axis=0), weight_split[...])
        total = (product[64:, 128:] + product[64:, :128]) + (product[:64, 128:] + product[:64, :128])
        tiles[step] = total.reshape(8, 8, 128)
        if step == FAR:
            pl.semaphore_wait(far_ready, 1)
        for offset in sum_peers(step):
            sum_copy(step, offset).start()

    @pl.when(early)
    def _():
        for index, step in enumerate(EARLY_ROUNDS):
            compute_round(step, EARLY_ROUNDS[:index])

    @pl.when(jnp.logical_not(early))
    def _():
        for index, step in enumerate(LATE_ROUNDS):
            compute_round(step, (HELD[FAR],) if index else ())

    pltpu.make_async_copy(right_got, right_got, right_send_sem).wait()
    pltpu.make_async_copy(sums, sums, sum_send_sem).wait()
    pltpu.make_async_copy(sums, sums, sum_recv_sem).wait()
    for step in range(ROUNDS):
        total = bias[...] if step == FAR else tiles[step, seq] + bias[...]
        for offset in sum_peers(step):
            total = total + sums[sum_slot(step, offset)]
        out_ref[step] = total


def on_device(features, gain, left_weight, right_weight, weight, bias):
    local_seqs, residues, channels = features.shape
    rows = local_seqs * residues
    f32, bf16 = jnp.float32, jnp.bfloat16
    dma = pltpu.SemaphoreType.DMA
    out = pl.pallas_call(
        kernel,
        out_shape=pltpu.VMEM((ROUNDS, 8, 128), f32),
        in_specs=[pl.BlockSpec(memory_space=pltpu.HBM)] * 6,
        out_specs=pl.BlockSpec(memory_space=pltpu.VMEM),
        scratch_shapes=[
            pltpu.VMEM((rows, channels), f32),
            pltpu.VMEM((1, channels), f32),
            pltpu.VMEM((32, channels), f32),
            pltpu.VMEM((32, channels), f32),
            pltpu.VMEM((1024, 128), f32),
            pltpu.VMEM((1, 128), f32),
            dma((6,)),
            pltpu.VMEM((256, channels), bf16),
            pltpu.VMEM((256, channels), bf16),
            pltpu.VMEM((1024, 256), bf16),
            pltpu.VMEM((rows, 128), f32),
            pltpu.VMEM((rows, 128), f32),
            pltpu.VMEM((256, 128), f32),
            pltpu.VMEM((256, 256), bf16),
            pltpu.VMEM((local_seqs, 256), f32),
            pltpu.VMEM((local_seqs, 256), f32),
            pltpu.VMEM((ROUNDS, local_seqs, 256), f32),
            pltpu.VMEM((256, 256), f32),
            pltpu.VMEM((ROUNDS, 8, 8, 128), f32),
            pltpu.VMEM((SUMS, 8, 128), f32),
            dma,
            dma((ROUNDS,)),
            dma,
            dma,
            pltpu.SemaphoreType.REGULAR,
            pltpu.SemaphoreType.REGULAR,
        ],
        compiler_params=pltpu.CompilerParams(
            collective_id=0, has_side_effects=True, vmem_limit_bytes=32 * 1024 * 1024
        ),
    )(
        *(
            pltpu.with_memory_space_constraint(operand, pltpu.HBM)
            for operand in (
                features.reshape(rows, channels),
                gain.reshape(1, channels),
                left_weight.T,
                right_weight.T,
                weight,
                bias.reshape(1, 128),
            )
        )
    )
    return out.reshape(ROUNDS, 8, 1, 128)


def solution(mesh):
    in_specs = (P("seq", "res", None), P(), P(), P(), P(), P())
    out_specs = P(None, "res", "seq", None)
    return jax.shard_map(
        on_device, mesh=mesh, in_specs=in_specs, out_specs=out_specs, check_vma=False
    )
```

```python
import jax
import jax.numpy as jnp
from jax import lax
from jax.experimental import pallas as pl
from jax.experimental.pallas import tpu as pltpu
from jax.sharding import PartitionSpec as P

ROUNDS = 4
EARLY_SENDS = (3, 2, 1, 0)
LATE_SENDS = (3, 1, 2, 0)
EARLY_ROUNDS = (0, 3, 1, 2)
LATE_ROUNDS = (2, 3, 1, 0)
MASKS = (1, 2, 6, 8)
HELD = (0, 1, 1, 3)
FAR = 2
SUMS = 29
NEAR_SLOT = (0, 1, None, 2)
PEERS = (6, 7, 4, 5, 2, 3, 1)
GREETED = (4, 5, 2, 3, 1)


def split(value):
    high = value.astype(jnp.bfloat16)
    low = (value - high.astype(jnp.float32)).astype(jnp.bfloat16)
    return high, low


def matmul(a, b):
    return lax.dot_general(a, b, (((1,), (0,)), ((), ())), preferred_element_type=jnp.float32)


def matmul_nt(a, b):
    return lax.dot_general(a, b, (((1,), (1,)), ((), ())), preferred_element_type=jnp.float32)


def group_index(rows, width):
    return lax.broadcasted_iota(jnp.int32, (rows, 128), 1) // width


def pick(parts, group):
    result = parts[-1]
    for index in range(len(parts) - 2, -1, -1):
        result = jnp.where(group == index, parts[index], result)
    return result


def kernel(
    features_hbm,
    gain_hbm,
    left_hbm,
    right_hbm,
    weight_hbm,
    bias_hbm,
    out_ref,
    features,
    gain,
    left_weight,
    right_weight,
    weight,
    bias,
    in_sem,
    proj_high,
    proj_low,
    weight_split,
    left_rows,
    right_rows,
    left_turned,
    left_parts,
    left_mine,
    right_mine,
    right_got,
    outer,
    tiles,
    sums,
    right_send_sem,
    right_recv_sem,
    sum_send_sem,
    sum_recv_sem,
    peers_ready,
    far_ready,
):
    rows = features.shape[0]
    local_seqs = rows // 8
    hidden = 32
    seq_devices = 8
    total_seqs = local_seqs * seq_devices

    block = lax.axis_index("res")
    seq = lax.axis_index("seq")

    def flip(index, mask):
        result = index
        for bit in (1, 2, 4, 8):
            if mask & bit:
                result = result + bit - 2 * bit * ((index // bit) % 2)
        return result

    def partner(step):
        return flip(block, MASKS[step])

    def peer(offset):
        return flip(seq, offset)

    def sum_peers(step):
        return PEERS + (0,) if step == FAR else PEERS

    copies = [
        pltpu.make_async_copy(source, target, in_sem.at[index])
        for index, (source, target) in enumerate(
            (
                (features_hbm, features),
                (left_hbm, left_weight),
                (right_hbm, right_weight),
                (gain_hbm, gain),
                (weight_hbm, weight),
                (bias_hbm, bias),
            )
        )
    ]
    for copy in copies:
        copy.start()

    barrier = pltpu.get_barrier_semaphore()
    for step in range(ROUNDS):
        pl.semaphore_signal(barrier, inc=1, device_id=(partner(step), seq))
    for offset in GREETED:
        pl.semaphore_signal(barrier, inc=1, device_id=(block, peer(offset)))

    for copy in copies[1:4]:
        copy.wait()
    left_high, left_low = split(left_weight[...] * gain[...])
    right_high, right_low = split(right_weight[...] * gain[...])
    proj_high[...] = jnp.concatenate([left_high] * 4 + [right_high] * 4, axis=0)
    proj_low[...] = jnp.concatenate([left_low] * 4 + [right_low] * 4, axis=0)

    def right_copy(step):
        return pltpu.make_async_remote_copy(
            src_ref=left_mine if step == FAR else right_mine,
            dst_ref=right_got.at[step],
            send_sem=right_send_sem,
            recv_sem=right_recv_sem.at[step],
            device_id=(partner(step), seq),
        )

    copies[0].wait()
    values = features[...]
    centered = values - jnp.mean(values, axis=1, keepdims=True)
    variance = jnp.mean(centered * centered, axis=1, keepdims=True)
    high, low = split(centered * lax.rsqrt(variance + 1e-05))
    projected = (
        matmul_nt(high, proj_low[...]) + matmul_nt(low, proj_high[...])
    ) + matmul_nt(high, proj_high[...])
    left_rows[...] = projected[:, :128]
    right_rows[...] = projected[:, 128:]
    seq_group = group_index(local_seqs, hidden)
    for source, target, scale in (
        (left_rows, left_mine, 1.0 / total_seqs),
        (right_rows, right_mine, 1.0),
    ):
        for half in range(2):
            lanes = [source[pl.ds(half * 4 + x, local_seqs, stride=8), :] for x in range(4)]
            target[:, pl.ds(half * 128, 128)] = pick(lanes, seq_group) * scale
    pl.semaphore_wait(barrier, ROUNDS + len(GREETED))
    early = block % 8 < 4

    @pl.when(early)
    def _():
        for step in EARLY_SENDS:
            right_copy(step).start()

    @pl.when(jnp.logical_not(early))
    def _():
        for step in LATE_SENDS:
            right_copy(step).start()

    for offset in GREETED:
        pl.semaphore_signal(peers_ready, inc=1, device_id=(block, peer(offset)))

    def turn_left(rows):
        for half in range(2):
            left_half = rows[:, half * 128 : half * 128 + 128]
            left_turned[pl.ds(half * 128, 128), :] = jnp.concatenate(
                [left_half, left_half], axis=0
            ).T
        left_columns = jnp.concatenate(
            [left_turned[pl.ds(c, 8, stride=hidden), :] for c in range(hidden)], axis=0
        )
        turned_high, turned_low = split(left_columns)
        return jnp.concatenate([turned_high, turned_low], axis=1)

    left_parts[...] = turn_left(left_mine[...])

    for copy in copies[4:]:
        copy.wait()
    weight_high, weight_low = split(weight[...])
    weight_split[...] = jnp.concatenate([weight_high, weight_low], axis=1)

    pl.semaphore_wait(peers_ready, len(GREETED))
    pl.semaphore_signal(far_ready, inc=1, device_id=(partner(FAR), seq))

    def sum_slot(step, offset):
        if step == FAR:
            return SUMS - seq_devices + offset
        return NEAR_SLOT[step] * (seq_devices - 1) + offset - 1

    def sum_copy(step, offset):
        return pltpu.make_async_remote_copy(
            src_ref=tiles.at[step, peer(offset)],
            dst_ref=sums.at[sum_slot(step, offset)],
            send_sem=sum_send_sem,
            recv_sem=sum_recv_sem,
            device_id=(partner(FAR) if step == FAR else block, peer(offset)),
        )

    group = group_index(8, hidden)
    def compute_round(step, arrived):
        if step not in arrived:
            right_copy(step).wait_recv()
        if step == FAR:
            left = turn_left(right_got[FAR])
            if HELD[FAR] not in arrived:
                right_copy(HELD[FAR]).wait_recv()
        else:
            left = left_parts[...]
        right_high, right_low = split(right_got[HELD[step]])
        outer[...] = matmul(
            left,
            jnp.concatenate([right_high, right_low, right_high, right_low], axis=0),
        )
        pieces = []
        for y_half in range(2):
            columns = [[None] * 8 for _ in range(4)]
            for c_quad in range(8):
                turned = [
                    outer[pl.ds((c_quad * 4 + i) * 8, 8), pl.ds(y_half * 128, 128)]
                    for i in range(4)
                ]
                turned = [turned[0]] + [pltpu.roll(turned[i], 32 * i, 1) for i in range(1, 4)]
                for y in range(4):
                    mixed = pick([turned[(g - y) % 4] for g in range(4)], group)
                    if y:
                        mixed = pltpu.roll(mixed, 128 - 32 * y, 1)
                    columns[y][c_quad] = mixed
            for y in range(4):
                pieces.append(jnp.concatenate(columns[y], axis=1))
        flat_high, flat_low = split(jnp.concatenate(pieces, axis=0))
        product = matmul(jnp.concatenate([flat_high, flat_low], axis=0), weight_split[...])
        total = (product[64:, 128:] + product[64:, :128]) + (product[:64, 128:] + product[:64, :128])
        tiles[step] = total.reshape(8, 8, 128)
        if step == FAR:
            pl.semaphore_wait(far_ready, 1)
        for offset in sum_peers(step):
            sum_copy(step, offset).start()

    @pl.when(early)
    def _():
        for index, step in enumerate(EARLY_ROUNDS):
            compute_round(step, EARLY_ROUNDS[:index])

    @pl.when(jnp.logical_not(early))
    def _():
        for index, step in enumerate(LATE_ROUNDS):
            compute_round(step, (HELD[FAR],) if index else ())

    pltpu.make_async_copy(right_got, right_got, right_send_sem).wait()
    pltpu.make_async_copy(sums, sums, sum_send_sem).wait()
    pltpu.make_async_copy(sums, sums, sum_recv_sem).wait()
    for step in range(ROUNDS):
        total = bias[...] if step == FAR else tiles[step, seq] + bias[...]
        for offset in sum_peers(step):
            total = total + sums[sum_slot(step, offset)]
        out_ref[step] = total


def on_device(features, gain, left_weight, right_weight, weight, bias):
    local_seqs, residues, channels = features.shape
    rows = local_seqs * residues
    f32, bf16 = jnp.float32, jnp.bfloat16
    dma = pltpu.SemaphoreType.DMA
    out = pl.pallas_call(
        kernel,
        out_shape=pltpu.VMEM((ROUNDS, 8, 128), f32),
        in_specs=[pl.BlockSpec(memory_space=pltpu.HBM)] * 6,
        out_specs=pl.BlockSpec(memory_space=pltpu.VMEM),
        scratch_shapes=[
            pltpu.VMEM((rows, channels), f32),
            pltpu.VMEM((1, channels), f32),
            pltpu.VMEM((32, channels), f32),
            pltpu.VMEM((32, channels), f32),
            pltpu.VMEM((1024, 128), f32),
            pltpu.VMEM((1, 128), f32),
            dma((6,)),
            pltpu.VMEM((256, channels), bf16),
            pltpu.VMEM((256, channels), bf16),
            pltpu.VMEM((1024, 256), bf16),
            pltpu.VMEM((rows, 128), f32),
            pltpu.VMEM((rows, 128), f32),
            pltpu.VMEM((256, 128), f32),
            pltpu.VMEM((256, 256), bf16),
            pltpu.VMEM((local_seqs, 256), f32),
            pltpu.VMEM((local_seqs, 256), f32),
            pltpu.VMEM((ROUNDS, local_seqs, 256), f32),
            pltpu.VMEM((256, 256), f32),
            pltpu.VMEM((ROUNDS, 8, 8, 128), f32),
            pltpu.VMEM((SUMS, 8, 128), f32),
            dma,
            dma((ROUNDS,)),
            dma,
            dma,
            pltpu.SemaphoreType.REGULAR,
            pltpu.SemaphoreType.REGULAR,
        ],
        compiler_params=pltpu.CompilerParams(
            collective_id=0, has_side_effects=True, vmem_limit_bytes=32 * 1024 * 1024
        ),
    )(
        *(
            pltpu.with_memory_space_constraint(operand, pltpu.HBM)
            for operand in (
                features.reshape(rows, channels),
                gain.reshape(1, channels),
                left_weight.T,
                right_weight.T,
                weight,
                bias.reshape(1, 128),
            )
        )
    )
    return out.reshape(ROUNDS, 8, 1, 128)


def solution(mesh):
    in_specs = (P("seq", "res", None), P(), P(), P(), P(), P())
    out_specs = P(None, "res", "seq", None)
    return jax.shard_map(
        on_device, mesh=mesh, in_specs=in_specs, out_specs=out_specs, check_vma=False
    )
```
